32 devices in a mesh: groups: 2 (over x), bx: 16 (over z, y, core).
Axes of the slice: x: 2, y: 2, z: 4, core: 2. Of those that a mesh axis runs over, the one named last changes fastest.
Arguments:
- rhs: bfloat16 [192, 512, 256], P(('groups', 'bx')), parts along dimension 0, may hold values from -6 to 6
- tiles: bfloat16 [4, 3, 192, 256, 256], P(None, None, ('groups', 'bx')), parts along dimension 2, may hold values from -0.1875 to 0.1875
- occupancy: int32 [192, 256], P(('groups', 'bx')), parts along dimension 0, may hold values 0 or 1
Outputs:
- applied: float32 [192, 512, 256], P(('groups', 'bx')), parts along dimension 0
The draws below stay inside these ranges and needn't reach their ends.
There are 2 independent parts, one for each index of `groups`. The reference program is written for one: setup_inputs(seed, part) draws one part's arguments, and reference() takes and returns one part's arrays. A program takes and returns all parts, laid end to end along the dimension named above; each array names one. Nothing has to cross between parts.
All inputs are finite; a program needn't handle non-finite values. No bound on the sum of `occupancy` on one device may be relied on, other than what follows from the above.
Results may differ from the reference program's by a relative error of at most 0.0026.
Values may be sent and summed in bfloat16 or wider, within the bound.
A program may use at most 64 MiB of HBM per device.

```python
import jax
import jax.numpy as jnp

R = 256
NRHS = 512
LEVELS = 3
BPD = 6
NB = 96
N_BX = 16


def plant(result, stream_key, smallest, high):
    longest = result.shape.index(max(result.shape))
    spots = []
    for shift in (0, 1):
        where = [jax.random.randint(jax.random.fold_in(stream_key, axis), (), 0, length) for axis, length in enumerate(result.shape)]
        where[longest] = (where[longest] + shift) % result.shape[longest]
        spots.append(tuple(where))
    return result.at[spots[0]].set(smallest).at[spots[1]].set(high)


def levels(key, shape, pieces, low, top_value):
    factor_of, own = 1.0, jax.random.fold_in(key, 6)
    for dim, shards_of in pieces:
        steps = jnp.exp(jax.random.uniform(jax.random.fold_in(own, dim), (shards_of,), jnp.float32, low / len(pieces), top_value / len(pieces)))
        factor_of = factor_of * jnp.repeat(steps, shape[dim] // shards_of).reshape([-1 if axis == dim else 1 for axis in range(len(shape))])
    return factor_of


def normal_values(rng, extent, deviation, most, split=(), held_as=jnp.bfloat16):
    level = levels(rng, extent, split, -0.22, 0.18) if split else 1.0
    values = jax.random.normal(rng, extent, jnp.float32) * deviation * level
    return jnp.minimum(jnp.maximum(values, -most), most).astype(held_as)


def setup_inputs(seed: int = 0, part: int = 0) -> dict:
    keys = jax.random.split(jax.random.key(seed), 4)
    part_splits = jax.random.split(jax.random.fold_in(keys[3], part), 4)
    rhs = normal_values(part_splits[0], (NB, NRHS, R), 1.0, 6.0, ((0, 16),))
    tiles = normal_values(part_splits[1], (4, LEVELS, NB, R, R), (4 * R) ** -0.5, 0.1875, ((2, 16),))
    occupancy = plant((jax.random.randint(part_splits[2], (NB, R), 0, 4) < 3).astype(jnp.int32), jax.random.fold_in(part_splits[2], 1), 0, 1)
    return dict(rhs=rhs, tiles=tiles, occupancy=occupancy)


def reference(rhs, tiles, occupancy):
    state = rhs.astype(jnp.float32)
    keep = occupancy.astype(jnp.float32)[:, None, :]
    owners = jnp.arange(N_BX, dtype=jnp.int32)
    for level in range(LEVELS):
        sent = state.astype(jnp.bfloat16)
        grid = sent.reshape(N_BX, BPD, NRHS, R)
        partner = grid[owners ^ (1 << level)].reshape(NB, NRHS, R)
        left = jnp.roll(grid, 1, axis=0).reshape(NB, NRHS, R)
        right = jnp.roll(grid, -1, axis=0).reshape(NB, NRHS, R)
        coupled = jnp.zeros((NB, NRHS, R), jnp.float32)
        for kind, source in enumerate((sent, partner, left, right)):
            coupled = coupled + jnp.einsum("bnr,brs->bns", source.astype(jnp.float32), tiles[kind, level].astype(jnp.float32))
        state = state + keep * coupled
    return state
```

```python
import functools

import jax
import jax.numpy as jnp
from jax import lax
from jax.experimental import pallas as pl
from jax.experimental.pallas import tpu as pltpu
from jax.sharding import PartitionSpec as P

LEVELS = 3
SPLIT = 2
LAG = 2
LEAD = 3

PAIR, RING, PARTNER = range(3)


def kernel(count, pieces, rhs, tiles, occ, out, weights, state, sent, pair, ring, partner,
           send_sem, recv_sem, rhs_sem, tile_sem, out_sem):
    me = lax.axis_index("bx")
    boxes = pieces // SPLIT
    even = lax.rem(me, 2) == 0
    inner = (lax.rem(me, 4) == 1) | (lax.rem(me, 4) == 2)

    def flipped(by):
        return jnp.where(lax.rem(me // by, 2) == 0, me + by, me - by)

    def along(by):
        return lax.rem(me + jnp.where(even, count - by, by), count)

    mate, across, beyond = flipped(1), flipped(2), flipped(4)
    neighbour, far = along(1), along(3)
    relay = jnp.where(inner, far, mate)
    mate_tile = jnp.where(even, 3, 2)

    def rhs_copy(i):
        return pltpu.make_async_copy(rhs.at[i], sent.at[0, i], rhs_sem.at[i])

    def tile_copy(level, k):
        return pltpu.make_async_copy(tiles.at[:, level, k], weights.at[level, k], tile_sem.at[level, k])

    def out_copy(i):
        return pltpu.make_async_copy(state.at[i], out.at[i], out_sem.at[i])

    def remote(level, kind, i):
        source = sent.at[level, i]
        if kind == PAIR:
            target, device = pair.at[level, i], mate
        elif kind == PARTNER:
            target, device = partner.at[level - 1, i], across if level == 1 else beyond
        else:
            target, device = ring.at[level, i], neighbour
            if level == 1:
                source, device = partner.at[0, i], relay
        return pltpu.make_async_remote_copy(
            src_ref=source,
            dst_ref=target,
            send_sem=send_sem.at[level, kind, i],
            recv_sem=recv_sem.at[level, kind, i],
            device_id={"bx": device},
            device_id_type=pl.DeviceIdType.MESH,
        )

    def send(level, i):
        if level > 0:
            remote(level, PARTNER, i).start()
        if level != 1:
            remote(level, RING, i).start()
        remote(level, PAIR, i).start()

    def forward(i):
        remote(1, PARTNER, i).wait_recv()
        remote(1, RING, i).start()

    def work(level, i):
        k = i // SPLIT

        @pl.when(lax.rem(i, SPLIT) == 0)
        def _():
            tile_copy(level, k).wait()

        remote(level, PAIR, i).wait_recv()
        remote(level, RING, i).wait_recv()
        if level == 2:
            remote(level, PARTNER, i).wait_recv()

        def product(source, kind):
            return jnp.dot(source, weights[level, k, kind], preferred_element_type=jnp.float32)

        own, beside = sent[level, i], pair[level, i]
        met = beside if level == 0 else partner[level - 1, i]
        coupled = product(own, 0) + product(met, 1)
        coupled = coupled + product(beside, mate_tile) + product(ring[level, i], 5 - mate_tile)
        keep = occ[pl.ds(k, 1), :].astype(jnp.float32)
        before = own.astype(jnp.float32) if level == 0 else state[i]
        after = before + keep * coupled
        state[i] = after
        if level < LEVELS - 1:
            sent[level + 1, i] = after.astype(jnp.bfloat16)
            send(level + 1, i)
        else:
            out_copy(i).start()

    def each(start, stop, step):
        def run(i, carry):
            step(i)
            return carry

        lax.fori_loop(start, stop, run, 0)

    each(0, pieces, lambda i: rhs_copy(i).start())
    barrier = pltpu.get_barrier_semaphore()
    for other in (mate, across, beyond, neighbour, far):
        pl.semaphore_signal(barrier, inc=1, device_id={"bx": other}, device_id_type=pl.DeviceIdType.MESH)
    for level in range(LEVELS):
        each(0, boxes, lambda k: tile_copy(level, k).start())
    each(0, pieces, lambda i: rhs_copy(i).wait())
    pl.semaphore_wait(barrier, 5)
    each(0, LEAD, lambda i: send(0, i))

    def step(s):
        def when_valid(i, action):
            @pl.when((i >= 0) & (i < pieces))
            def _():
                action(i)

        when_valid(s, lambda i: work(0, i))
        when_valid(s + LEAD, lambda i: send(0, i))
        when_valid(s - LAG + 1, forward)
        when_valid(s - LAG, lambda i: work(1, i))
        when_valid(s - 2 * LAG, lambda i: work(2, i))

    each(0, pieces + 2 * LAG, step)

    def finish(i):
        for level in range(LEVELS):
            for kind in (PAIR, RING, PARTNER):
                if level or kind != PARTNER:
                    remote(level, kind, i).wait_send()
        out_copy(i).wait()

    each(0, pieces, finish)


def body(count, rhs, tiles, occupancy):
    boxes, columns, rows = rhs.shape
    pieces, part = boxes * SPLIT, columns // SPLIT
    block = (pieces, part, rows)
    out = pl.pallas_call(
        functools.partial(kernel, count, pieces),
        out_shape=jax.ShapeDtypeStruct(block, jnp.float32),
        in_specs=[
            pl.BlockSpec(memory_space=pl.ANY),
            pl.BlockSpec(memory_space=pl.ANY),
            pl.BlockSpec(memory_space=pltpu.VMEM),
        ],
        out_specs=pl.BlockSpec(memory_space=pl.ANY),
        scratch_shapes=[
            pltpu.VMEM((LEVELS, boxes, 4, rows, rows), jnp.bfloat16),
            pltpu.VMEM(block, jnp.float32),
            pltpu.VMEM((LEVELS, *block), jnp.bfloat16),
            pltpu.VMEM((LEVELS, *block), jnp.bfloat16),
            pltpu.VMEM((LEVELS, *block), jnp.bfloat16),
            pltpu.VMEM((LEVELS - 1, *block), jnp.bfloat16),
            pltpu.SemaphoreType.DMA((LEVELS, 3, pieces)),
            pltpu.SemaphoreType.DMA((LEVELS, 3, pieces)),
            pltpu.SemaphoreType.DMA((pieces,)),
            pltpu.SemaphoreType.DMA((LEVELS, boxes)),
            pltpu.SemaphoreType.DMA((pieces,)),
        ],
        compiler_params=pltpu.CompilerParams(
            collective_id=0, has_side_effects=True, vmem_limit_bytes=56 << 20
        ),
        cost_estimate=pl.CostEstimate(
            flops=8 * LEVELS * boxes * columns * rows * rows,
            bytes_accessed=2 * tiles.size + 6 * rhs.size,
            transcendentals=0,
        ),
    )(rhs.reshape(block), tiles, occupancy)
    return out.reshape(boxes, columns, rows)


def solution(mesh):
    placed = (
        P(("groups", "bx"), None, None),
        P(None, None, ("groups", "bx"), None, None),
        P(("groups", "bx"), None),
    )
    return jax.shard_map(
        functools.partial(body, mesh.shape["bx"]),
        mesh=mesh,
        in_specs=placed,
        out_specs=P(("groups", "bx"), None, None),
        check_vma=False,
    )
```

```python
import functools

import jax
import jax.numpy as jnp
from jax import lax
from jax.experimental import pallas as pl
from jax.experimental.pallas import tpu as pltpu
from jax.sharding import PartitionSpec as P

LEVELS = 3
SPLIT = 2
LAG = 2
LEAD = 2

PAIR, RING, PARTNER = range(3)


def kernel(count, pieces, rhs, tiles, occ, state, weights, sent, pair, ring, partner,
           send_sem, recv_sem, rhs_sem, tile_sem):
    me = lax.axis_index("bx")
    boxes = pieces // SPLIT
    even = lax.rem(me, 2) == 0
    inner = (lax.rem(me, 4) == 1) | (lax.rem(me, 4) == 2)

    def flipped(by):
        return jnp.where(lax.rem(me // by, 2) == 0, me + by, me - by)

    def along(by):
        return lax.rem(me + jnp.where(even, count - by, by), count)

    mate, across, beyond = flipped(1), flipped(2), flipped(4)
    neighbour, far = along(1), along(3)
    relay = jnp.where(inner, far, mate)
    mate_tile = jnp.where(even, 3, 2)

    def rhs_copy(i):
        return pltpu.make_async_copy(rhs.at[i], sent.at[0, i], rhs_sem.at[i])

    def tile_copy(level, k):
        return pltpu.make_async_copy(tiles.at[:, level, k], weights.at[level, k], tile_sem.at[level, k])

    def remote(level, kind, i):
        source = sent.at[level, i]
        if kind == PAIR:
            target, device = pair.at[level, i], mate
        elif kind == PARTNER:
            target, device = partner.at[level - 1, i], across if level == 1 else beyond
        else:
            target, device = ring.at[level, i], neighbour
            if level == 1:
                source, device = partner.at[0, i], relay
        return pltpu.make_async_remote_copy(
            src_ref=source,
            dst_ref=target,
            send_sem=send_sem.at[level, kind, i],
            recv_sem=recv_sem.at[level, kind, i],
            device_id={"bx": device},
            device_id_type=pl.DeviceIdType.MESH,
        )

    def send(level, i):
        if level > 0:
            remote(level, PARTNER, i).start()
        if level != 1:
            remote(level, RING, i).start()
        remote(level, PAIR, i).start()

    def forward(i):
        remote(1, PARTNER, i).wait_recv()
        remote(1, RING, i).start()

    def work(level, i):
        k = i // SPLIT

        @pl.when(lax.rem(i, SPLIT) == 0)
        def _():
            tile_copy(level, k).wait()

        remote(level, PAIR, i).wait_recv()
        remote(level, RING, i).wait_recv()
        if level == 2:
            remote(level, PARTNER, i).wait_recv()

        def product(source, kind):
            return jnp.dot(source, weights[level, k, kind], preferred_element_type=jnp.float32)

        own, beside = sent[level, i], pair[level, i]
        met = beside if level == 0 else partner[level - 1, i]
        coupled = product(own, 0) + product(met, 1)
        coupled = coupled + product(beside, mate_tile) + product(ring[level, i], 5 - mate_tile)
        keep = occ[pl.ds(k, 1), :].astype(jnp.float32)
        before = own.astype(jnp.float32) if level == 0 else state[i]
        after = before + keep * coupled
        state[i] = after
        if level < LEVELS - 1:
            sent[level + 1, i] = after.astype(jnp.bfloat16)
            send(level + 1, i)

    def each(start, stop, step):
        def run(i, carry):
            step(i)
            return carry

        lax.fori_loop(start, stop, run, 0)

    each(0, pieces, lambda i: rhs_copy(i).start())
    barrier = pltpu.get_barrier_semaphore()
    for other in (mate, across, beyond, neighbour, far):
        pl.semaphore_signal(barrier, inc=1, device_id={"bx": other}, device_id_type=pl.DeviceIdType.MESH)
    for level in range(LEVELS):
        each(0, boxes, lambda k: tile_copy(level, k).start())
    each(0, pieces, lambda i: rhs_copy(i).wait())
    pl.semaphore_wait(barrier, 5)
    each(0, LEAD, lambda i: send(0, i))

    def step(s):
        def when_valid(i, action):
            @pl.when((i >= 0) & (i < pieces))
            def _():
                action(i)

        when_valid(s, lambda i: work(0, i))
        when_valid(s + LEAD, lambda i: send(0, i))
        when_valid(s - LAG + 1, forward)
        when_valid(s - LAG, lambda i: work(1, i))
        when_valid(s - 2 * LAG, lambda i: work(2, i))

    each(0, pieces + 2 * LAG, step)

    def finish(i):
        for level in range(LEVELS):
            for kind in (PAIR, RING, PARTNER):
                if level or kind != PARTNER:
                    remote(level, kind, i).wait_send()

    each(0, pieces, finish)


def body(count, rhs, tiles, occupancy):
    boxes, columns, rows = rhs.shape
    pieces, part = boxes * SPLIT, columns // SPLIT
    block = (pieces, part, rows)
    out = pl.pallas_call(
        functools.partial(kernel, count, pieces),
        out_shape=pltpu.VMEM(block, jnp.float32),
        in_specs=[
            pl.BlockSpec(memory_space=pl.ANY),
            pl.BlockSpec(memory_space=pl.ANY),
            pl.BlockSpec(memory_space=pltpu.VMEM),
        ],
        out_specs=pl.BlockSpec(memory_space=pltpu.VMEM),
        scratch_shapes=[
            pltpu.VMEM((LEVELS, boxes, 4, rows, rows), jnp.bfloat16),
            pltpu.VMEM((LEVELS, *block), jnp.bfloat16),
            pltpu.VMEM((LEVELS, *block), jnp.bfloat16),
            pltpu.VMEM((LEVELS, *block), jnp.bfloat16),
            pltpu.VMEM((LEVELS - 1, *block), jnp.bfloat16),
            pltpu.SemaphoreType.DMA((LEVELS, 3, pieces)),
            pltpu.SemaphoreType.DMA((LEVELS, 3, pieces)),
            pltpu.SemaphoreType.DMA((pieces,)),
            pltpu.SemaphoreType.DMA((LEVELS, boxes)),
        ],
        compiler_params=pltpu.CompilerParams(
            collective_id=0, has_side_effects=True, vmem_limit_bytes=56 << 20
        ),
        cost_estimate=pl.CostEstimate(
            flops=8 * LEVELS * boxes * columns * rows * rows,
            bytes_accessed=2 * tiles.size + 6 * rhs.size,
            transcendentals=0,
        ),
    )(rhs.reshape(block), tiles, occupancy)
    return out.reshape(boxes, columns, rows)


def solution(mesh):
    placed = (
        P(("groups", "bx"), None, None),
        P(None, None, ("groups", "bx"), None, None),
        P(("groups", "bx"), None),
    )
    return jax.shard_map(
        functools.partial(body, mesh.shape["bx"]),
        mesh=mesh,
        in_specs=placed,
        out_specs=P(("groups", "bx"), None, None),
        check_vma=False,
    )
```

```python
import functools

import jax
import jax.numpy as jnp
from jax import lax
from jax.experimental import pallas as pl
from jax.experimental.pallas import tpu as pltpu
from jax.sharding import PartitionSpec as P

LEVELS = 3
SPLIT = 2
LAG_MIDDLE = 2
LAG_LAST = 7
RELAY = 1
LEAD = 2

PAIR, RING, PARTNER = range(3)


def kernel(count, pieces, rhs, tiles, occ, state, weights, sent, pair, ring, partner,
           send_sem, recv_sem, rhs_sem, tile_sem):
    me = lax.axis_index("bx")
    boxes = pieces // SPLIT
    even = lax.rem(me, 2) == 0
    inner = (lax.rem(me, 4) == 1) | (lax.rem(me, 4) == 2)

    def flipped(by):
        return jnp.where(lax.rem(me // by, 2) == 0, me + by, me - by)

    def along(by):
        return lax.rem(me + jnp.where(even, count - by, by), count)

    mate, across, beyond = flipped(1), flipped(2), flipped(4)
    neighbour, far = along(1), along(3)
    relay = jnp.where(inner, far, mate)
    mate_tile = jnp.where(even, 3, 2)

    def rhs_copy(i):
        return pltpu.make_async_copy(rhs.at[i], sent.at[0, i], rhs_sem.at[i])

    def tile_copy(level, k):
        return pltpu.make_async_copy(tiles.at[:, level, k], weights.at[level, k], tile_sem.at[level, k])

    def remote(level, kind, i):
        source = sent.at[level, i]
        if kind == PAIR:
            target, device = pair.at[level, i], mate
        elif kind == PARTNER:
            target, device = partner.at[level - 1, i], across if level == 1 else beyond
        else:
            target, device = ring.at[level, i], neighbour
            if level == 1:
                source, device = partner.at[0, i], relay
        return pltpu.make_async_remote_copy(
            src_ref=source,
            dst_ref=target,
            send_sem=send_sem.at[level, kind, i],
            recv_sem=recv_sem.at[level, kind, i],
            device_id={"bx": device},
            device_id_type=pl.DeviceIdType.MESH,
        )

    def send(level, i):
        if level > 0:
            remote(level, PARTNER, i).start()
        if level != 1:
            remote(level, RING, i).start()
        remote(level, PAIR, i).start()

    def forward(i):
        remote(1, PARTNER, i).wait_recv()
        remote(1, RING, i).start()

    def work(level, i):
        k = i // SPLIT

        @pl.when(lax.rem(i, SPLIT) == 0)
        def _():
            tile_copy(level, k).wait()

        remote(level, PAIR, i).wait_recv()
        remote(level, RING, i).wait_recv()
        if level == 2:
            remote(level, PARTNER, i).wait_recv()

        def product(source, kind):
            return jnp.dot(source, weights[level, k, kind], preferred_element_type=jnp.float32)

        own, beside = sent[level, i], pair[level, i]
        met = beside if level == 0 else partner[level - 1, i]
        coupled = product(own, 0) + product(met, 1)
        coupled = coupled + product(beside, mate_tile) + product(ring[level, i], 5 - mate_tile)
        keep = occ[pl.ds(k, 1), :].astype(jnp.float32)
        before = own.astype(jnp.float32) if level == 0 else state[i]
        after = before + keep * coupled
        state[i] = after
        if level < LEVELS - 1:
            sent[level + 1, i] = after.astype(jnp.bfloat16)
            send(level + 1, i)

    def each(start, stop, step):
        def run(i, carry):
            step(i)
            return carry

        lax.fori_loop(start, stop, run, 0)

    barrier = pltpu.get_barrier_semaphore()
    for other in (far, neighbour, beyond, across, mate):
        pl.semaphore_signal(barrier, inc=1, device_id={"bx": other}, device_id_type=pl.DeviceIdType.MESH)
    each(0, pieces, lambda i: rhs_copy(i).start())
    for level in range(LEVELS):
        each(0, boxes, lambda k: tile_copy(level, k).start())
    each(0, pieces, lambda i: rhs_copy(i).wait())
    pl.semaphore_wait(barrier, 5)
    each(0, LEAD, lambda i: send(0, i))

    def step(s):
        def when_valid(i, action):
            @pl.when((i >= 0) & (i < pieces))
            def _():
                action(i)

        when_valid(s, lambda i: work(0, i))
        when_valid(s + LEAD, lambda i: send(0, i))
        when_valid(s - RELAY, forward)
        when_valid(s - LAG_MIDDLE, lambda i: work(1, i))
        when_valid(s - LAG_LAST, lambda i: work(2, i))

    each(0, pieces + LAG_LAST, step)

    def finish(i):
        for level in range(LEVELS):
            for kind in (PAIR, RING, PARTNER):
                if level or kind != PARTNER:
                    remote(level, kind, i).wait_send()

    each(0, pieces, finish)


def body(count, rhs, tiles, occupancy):
    boxes, columns, rows = rhs.shape
    pieces, part = boxes * SPLIT, columns // SPLIT
    block = (pieces, part, rows)
    out = pl.pallas_call(
        functools.partial(kernel, count, pieces),
        out_shape=pltpu.VMEM(block, jnp.float32),
        in_specs=[
            pl.BlockSpec(memory_space=pl.ANY),
            pl.BlockSpec(memory_space=pl.ANY),
            pl.BlockSpec(memory_space=pltpu.VMEM),
        ],
        out_specs=pl.BlockSpec(memory_space=pltpu.VMEM),
        scratch_shapes=[
            pltpu.VMEM((LEVELS, boxes, 4, rows, rows), jnp.bfloat16),
            pltpu.VMEM((LEVELS, *block), jnp.bfloat16),
            pltpu.VMEM((LEVELS, *block), jnp.bfloat16),
            pltpu.VMEM((LEVELS, *block), jnp.bfloat16),
            pltpu.VMEM((LEVELS - 1, *block), jnp.bfloat16),
            pltpu.SemaphoreType.DMA((LEVELS, 3, pieces)),
            pltpu.SemaphoreType.DMA((LEVELS, 3, pieces)),
            pltpu.SemaphoreType.DMA((pieces,)),
            pltpu.SemaphoreType.DMA((LEVELS, boxes)),
        ],
        compiler_params=pltpu.CompilerParams(
            collective_id=0, has_side_effects=True, vmem_limit_bytes=56 << 20
        ),
        cost_estimate=pl.CostEstimate(
            flops=8 * LEVELS * boxes * columns * rows * rows,
            bytes_accessed=2 * tiles.size + 6 * rhs.size,
            transcendentals=0,
        ),
    )(rhs.reshape(block), tiles, occupancy)
    return out.reshape(boxes, columns, rows)


def solution(mesh):
    placed = (
        P(("groups", "bx"), None, None),
        P(None, None, ("groups", "bx"), None, None),
        P(("groups", "bx"), None),
    )
    return jax.shard_map(
        functools.partial(body, mesh.shape["bx"]),
        mesh=mesh,
        in_specs=placed,
        out_specs=P(("groups", "bx"), None, None),
        check_vma=False,
    )
```

```python
import functools

import jax
import jax.numpy as jnp
from jax import lax
from jax.experimental import pallas as pl
from jax.experimental.pallas import tpu as pltpu
from jax.sharding import PartitionSpec as P

LEVELS = 3
SPLIT = 2
LAG_MIDDLE = 2
LAG_LAST = 7
RELAY = 1
LEAD = 2

PAIR, RING, PARTNER = range(3)


def kernel(count, pieces, rhs, tiles, occ, state, weights, sent, pair, ring, partner,
           send_sem, recv_sem, rhs_sem, tile_sem):
    me = lax.axis_index("bx")
    boxes = pieces // SPLIT
    even = lax.rem(me, 2) == 0
    inner = (lax.rem(me, 4) == 1) | (lax.rem(me, 4) == 2)

    def flipped(by):
        return jnp.where(lax.rem(me // by, 2) == 0, me + by, me - by)

    def along(by):
        return lax.rem(me + jnp.where(even, count - by, by), count)

    mate, across, beyond = flipped(1), flipped(2), flipped(4)
    neighbour, far = along(1), along(3)
    relay = jnp.where(inner, far, mate)
    mate_tile = jnp.where(even, 3, 2)

    def rhs_copy(i):
        return pltpu.make_async_copy(rhs.at[i], sent.at[0, i], rhs_sem.at[i])

    def tile_copy(level, k):
        return pltpu.make_async_copy(tiles.at[:, level, k], weights.at[level, k], tile_sem.at[level, k])

    def remote(level, kind, i):
        source = sent.at[level, i]
        if kind == PAIR:
            target, device = pair.at[level, i], mate
        elif kind == PARTNER:
            target, device = partner.at[level - 1, i], across if level == 1 else beyond
        else:
            target, device = ring.at[level, i], neighbour
            if level == 1:
                source, device = partner.at[0, i], relay
        return pltpu.make_async_remote_copy(
            src_ref=source,
            dst_ref=target,
            send_sem=send_sem.at[level, kind, i],
            recv_sem=recv_sem.at[level, kind, i],
            device_id={"bx": device},
            device_id_type=pl.DeviceIdType.MESH,
        )

    def send(level, i):
        if level > 0:
            remote(level, PARTNER, i).start()
        if level != 1:
            remote(level, RING, i).start()
        remote(level, PAIR, i).start()

    def forward(i):
        remote(1, PARTNER, i).wait_recv()
        remote(1, RING, i).start()

    def work(level, i):
        k = i // SPLIT

        @pl.when(lax.rem(i, SPLIT) == 0)
        def _():
            tile_copy(level, k).wait()

        remote(level, PAIR, i).wait_recv()
        remote(level, RING, i).wait_recv()
        if level == 2:
            remote(level, PARTNER, i).wait_recv()

        def product(source, kind):
            return jnp.dot(source, weights[level, k, kind], preferred_element_type=jnp.float32)

        own, beside = sent[level, i], pair[level, i]
        met = beside if level == 0 else partner[level - 1, i]
        coupled = product(own, 0) + product(met, 1)
        coupled = coupled + product(beside, mate_tile) + product(ring[level, i], 5 - mate_tile)
        keep = occ[pl.ds(k, 1), :].astype(jnp.float32)
        before = own.astype(jnp.float32) if level == 0 else state[i]
        after = before + keep * coupled
        state[i] = after
        if level < LEVELS - 1:
            sent[level + 1, i] = after.astype(jnp.bfloat16)
            send(level + 1, i)

    def finish(i):
        for level in range(LEVELS):
            for kind in (PAIR, RING, PARTNER):
                if level or kind != PARTNER:
                    remote(level, kind, i).wait_send()

    def each(start, stop, step):
        def run(i, carry):
            step(i)
            return carry

        lax.fori_loop(start, stop, run, 0)

    barrier = pltpu.get_barrier_semaphore()
    for other in (far, neighbour, beyond, across, mate):
        pl.semaphore_signal(barrier, inc=1, device_id={"bx": other}, device_id_type=pl.DeviceIdType.MESH)
    each(0, pieces, lambda i: rhs_copy(i).start())
    for level in range(LEVELS):
        each(0, boxes, lambda k: tile_copy(level, k).start())
    each(0, pieces, lambda i: rhs_copy(i).wait())
    pl.semaphore_wait(barrier, 5)
    each(0, LEAD, lambda i: send(0, i))

    def step(s):
        def when_valid(i, action):
            @pl.when((i >= 0) & (i < pieces))
            def _():
                action(i)

        when_valid(s, lambda i: work(0, i))
        when_valid(s + LEAD, lambda i: send(0, i))
        when_valid(s - RELAY, forward)
        when_valid(s - LAG_MIDDLE, lambda i: work(1, i))
        when_valid(s - LAG_LAST, finish)
        when_valid(s - LAG_LAST, lambda i: work(2, i))

    each(0, pieces + LAG_LAST, step)


def body(count, rhs, tiles, occupancy):
    boxes, columns, rows = rhs.shape
    pieces, part = boxes * SPLIT, columns // SPLIT
    block = (pieces, part, rows)
    out = pl.pallas_call(
        functools.partial(kernel, count, pieces),
        out_shape=pltpu.VMEM(block, jnp.float32),
        in_specs=[
            pl.BlockSpec(memory_space=pl.ANY),
            pl.BlockSpec(memory_space=pl.ANY),
            pl.BlockSpec(memory_space=pltpu.VMEM),
        ],
        out_specs=pl.BlockSpec(memory_space=pltpu.VMEM),
        scratch_shapes=[
            pltpu.VMEM((LEVELS, boxes, 4, rows, rows), jnp.bfloat16),
            pltpu.VMEM((LEVELS, *block), jnp.bfloat16),
            pltpu.VMEM((LEVELS, *block), jnp.bfloat16),
            pltpu.VMEM((LEVELS, *block), jnp.bfloat16),
            pltpu.VMEM((LEVELS - 1, *block), jnp.bfloat16),
            pltpu.SemaphoreType.DMA((LEVELS, 3, pieces)),
            pltpu.SemaphoreType.DMA((LEVELS, 3, pieces)),
            pltpu.SemaphoreType.DMA((pieces,)),
            pltpu.SemaphoreType.DMA((LEVELS, boxes)),
        ],
        compiler_params=pltpu.CompilerParams(
            collective_id=0, has_side_effects=True, vmem_limit_bytes=56 << 20
        ),
        cost_estimate=pl.CostEstimate(
            flops=8 * LEVELS * boxes * columns * rows * rows,
            bytes_accessed=2 * tiles.size + 6 * rhs.size,
            transcendentals=0,
        ),
    )(rhs.reshape(block), tiles, occupancy)
    return out.reshape(boxes, columns, rows)


def solution(mesh):
    placed = (
        P(("groups", "bx"), None, None),
        P(None, None, ("groups", "bx"), None, None),
        P(("groups", "bx"), None),
    )
    return jax.shard_map(
        functools.partial(body, mesh.shape["bx"]),
        mesh=mesh,
        in_specs=placed,
        out_specs=P(("groups", "bx"), None, None),
        check_vma=False,
    )
```
